256 devices in a mesh: gx: 16 (over z_hi, x), gy: 16 (over y, z_lo, core).
Axes of the slice: x: 4, y: 4, z: 8 (z_hi: 4, z_lo: 2; z = z_hi * 2 + z_lo), core: 2. Of those that a mesh axis runs over, the one named last changes fastest.
Arguments:
- noise: bfloat16 [1024, 1024, 128], P('gy', 'gx'), may hold values from -6 to 6
- cheb_coeff: float32 [6], replicated, may hold values from 0.4 to 1.2
- diag_x: float32 [1024, 64], P('gx'), may hold values from -0.165 to 0.165
- couple_x: bfloat16 [1024, 64], P('gx'), may hold values from -0.1640625 to 0.1640625
- diag_y: float32 [1024, 64], P('gy'), may hold values from -0.165 to 0.165
- couple_y: bfloat16 [1024, 64], P('gy'), may hold values from -0.1640625 to 0.1640625
- track_rows: int32 [128], P('gy'), may hold values from 0 to 1023, as said below
- track_obs: float32 [128, 1024], P('gy', 'gx'), may hold values from -6 to 6
- weights: float32 [1024, 128], P('gy'), may hold values from -0.5 to 0.5
Outputs:
- conditioned: float32 [1024, 1024, 128], P('gy', 'gx')
The draws below stay inside these ranges and needn't reach their ends.
Inputs may be any that keep to these rules, and one draw needn't show every extreme that they name: `track_rows`: in block j of 8 entries (j from 0) the entries are distinct rows of j * 64 to j * 64 + 63; the block's first entry is its first row where j is even and its last row where j is odd.
All inputs are finite; a program needn't handle non-finite values.
Results may differ from the reference program's by a relative error of at most 0.0055.
Values may be sent and summed in bfloat16 or wider, within the bound.
No kernel may reach another device: no remote copies, remote signals or barrier semaphores. Data moves between devices by JAX's collectives and lax.ppermute only.
A program may use at most 64 MiB of HBM per device.

```python
import jax
import jax.numpy as jnp
from jax import lax

BLK = 64
SAMPLES = 128
TERMS = 6
TRK_DEV = 8
NX = 1024
NY = 1024
TRACKS = 128


def draw_track_rows(key, part):
    groups = TRACKS // TRK_DEV
    keys = jax.random.split(key, groups)

    def pick_rows(one_key):
        return jax.random.permutation(one_key, BLK - 2)[:TRK_DEV - 1]
    picks = jax.vmap(pick_rows)(keys).astype(jnp.int32) + 1
    index = jnp.arange(groups, dtype=jnp.int32)
    edge = index % 2 * (BLK - 1)
    rows = jnp.concatenate([edge[:, None], picks], axis=1) + index[:, None] * BLK
    return rows.reshape(-1).astype(jnp.int32)


def shard_levels(rng, dims, shards, low, largest):
    def one(axis_at, blocks):
        steps = jax.random.uniform(jax.random.fold_in(jax.random.fold_in(rng, 6), axis_at), (blocks,), jnp.float32, low / len(shards), largest / len(shards))
        return jnp.repeat(jnp.exp(steps), dims[axis_at] // blocks).reshape((-1,) + (1,) * (len(dims) - axis_at - 1))

    level = one(*shards[0])
    for cut in shards[1:]:
        level = level * one(*cut)
    return level


def normal_values(stream_key, extent, scale, reach, pieces=(), kind=jnp.bfloat16):
    entries = scale * jax.random.normal(stream_key, extent, jnp.float32)
    if pieces:
        entries = entries * shard_levels(stream_key, extent, pieces, -0.22, 0.18)
    return jnp.clip(entries, -reach, reach).astype(kind)


def setup_inputs(seed: int = 0) -> dict:
    seeds = jax.random.split(jax.random.key(seed), 10)
    noise = normal_values(seeds[0], (NY, NX, SAMPLES), 1.0, 6.0, ((0, 16), (1, 16)))
    cheb_coeff = jnp.clip(jax.random.uniform(seeds[1], (TERMS,), jnp.float32, 0.4, 1.2), 0.4, 1.2)
    diag_x = normal_values(seeds[2], (NX, BLK), (0.22 / BLK ** 0.5), 0.165, ((0, 16),), jnp.float32)
    couple_x = normal_values(seeds[3], (NX, BLK), (0.22 / BLK ** 0.5), 0.1640625, ((0, 16),))
    diag_y = normal_values(seeds[4], (NY, BLK), (0.22 / BLK ** 0.5), 0.165, ((0, 16),), jnp.float32)
    couple_y = normal_values(seeds[5], (NY, BLK), (0.22 / BLK ** 0.5), 0.1640625, ((0, 16),))
    track_rows = draw_track_rows(jax.random.fold_in(seeds[9], 71), 0)
    track_obs = normal_values(seeds[7], (TRACKS, NX), 1.0, 6.0, ((0, 16), (1, 16)), jnp.float32)
    weights = normal_values(seeds[8], (NY, TRACKS), TRACKS ** -0.5, 0.5, ((0, 16),), jnp.float32)
    return {"noise": noise, "cheb_coeff": cheb_coeff, "diag_x": diag_x, "couple_x": couple_x, "diag_y": diag_y, "couple_y": couple_y, "track_rows": track_rows, "track_obs": track_obs, "weights": weights}


NUGGET = 0.3


def round_keep(values):
    held = lax.optimization_barrier(values.astype(jnp.bfloat16))
    return held.astype(jnp.float32)


def apply_rows(field, diag_x, couple_x):
    xblocks = NX // BLK
    shaped = field.reshape(NY, xblocks, BLK, SAMPLES)
    inner = diag_x.reshape(xblocks, BLK, BLK)
    links = couple_x.reshape(xblocks, BLK, BLK).astype(jnp.float32)
    own = NUGGET * shaped + jnp.einsum("bij,ybjs->ybis", inner, shaped, precision=lax.Precision.HIGHEST)
    rounded = round_keep(shaped)
    empty = jnp.zeros((NY, 1, BLK, SAMPLES), jnp.float32)
    from_prev = jnp.einsum("bij,ybjs->ybis", links[1:], rounded[:, :-1], precision=lax.Precision.HIGHEST)
    from_next = jnp.einsum("bji,ybjs->ybis", links[1:], rounded[:, 1:], precision=lax.Precision.HIGHEST)
    from_prev = jnp.concatenate([empty, round_keep(from_prev)], axis=1)
    from_next = jnp.concatenate([round_keep(from_next), empty], axis=1)
    return (own + from_prev + from_next).reshape(NY, NX, SAMPLES)


def apply_cols(field, diag_y, couple_y):
    yblocks = NY // BLK
    shaped = field.reshape(yblocks, BLK, NX, SAMPLES)
    inner = diag_y.reshape(yblocks, BLK, BLK)
    links = couple_y.reshape(yblocks, BLK, BLK).astype(jnp.float32)
    own = NUGGET * shaped + jnp.einsum("bij,bjxs->bixs", inner, shaped, precision=lax.Precision.HIGHEST)
    rounded = round_keep(shaped)
    empty = jnp.zeros((1, BLK, NX, SAMPLES), jnp.float32)
    from_prev = jnp.einsum("bij,bjxs->bixs", links[1:], rounded[:-1], precision=lax.Precision.HIGHEST)
    from_next = jnp.einsum("bji,bjxs->bixs", links[1:], rounded[1:], precision=lax.Precision.HIGHEST)
    from_prev = jnp.concatenate([empty, round_keep(from_prev)], axis=0)
    from_next = jnp.concatenate([round_keep(from_next), empty], axis=0)
    return (own + from_prev + from_next).reshape(NY, NX, SAMPLES)


def reference(noise, cheb_coeff, diag_x, couple_x, diag_y, couple_y, track_rows, track_obs, weights):
    def operator(field):
        return apply_cols(apply_rows(field, diag_x, couple_x), diag_y, couple_y)

    start = noise.astype(jnp.float32)
    previous = start
    current = operator(start)
    total = cheb_coeff[0] * start
    total = total + cheb_coeff[1] * current
    for term in range(2, TERMS):
        following = 2.0 * operator(current) - previous
        previous = current
        current = following
        total = total + cheb_coeff[term] * current
    picked = jnp.take(total, track_rows.astype(jnp.int32), axis=0)
    misfit = picked - track_obs[:, :, None]
    correction = jnp.dot(weights, misfit.reshape(TRACKS, NX * SAMPLES), precision=lax.Precision.HIGHEST)
    return total - correction.reshape(NY, NX, SAMPLES)
```

```python
import jax
import jax.numpy as jnp
from jax import lax
from jax.experimental import pallas as pl
from jax.experimental.pallas import tpu as pltpu
from jax.sharding import Mesh, PartitionSpec as P

NUGGET = 0.3
BLK = 64
HALF = 32
N = 1024
S = 128
TILE = 256
TILES = N // TILE
BLOCKS = N // BLK
F32 = jnp.float32
BF16 = jnp.bfloat16
VMEM = pltpu.VMEM
SMEM = pltpu.SMEM


def low_lanes(shape):
    return lax.broadcasted_iota(jnp.int32, shape, len(shape) - 1) < BLK


def swap_halves(value):
    return pltpu.roll(value, BLK, axis=1)


def split_samples_kernel(noise_ref, out_ref, tmp_ref):
    for k in range(HALF):
        pair = jnp.concatenate([noise_ref[k], noise_ref[HALF + k]], axis=0).astype(F32)
        tmp_ref[pl.ds(k, S, stride=HALF), :] = pair.T
    out_ref[...] = tmp_ref[...].reshape(S, HALF, S).astype(BF16)


def split_samples(noise):
    return pl.pallas_call(
        split_samples_kernel,
        out_shape=jax.ShapeDtypeStruct((S, HALF, S), BF16),
        in_specs=[pl.BlockSpec(memory_space=VMEM)],
        out_specs=pl.BlockSpec(memory_space=VMEM),
        scratch_shapes=[VMEM((S * HALF, S), F32)],
        compiler_params=pltpu.CompilerParams(vmem_limit_bytes=32 * 1024 * 1024),
        cost_estimate=pl.CostEstimate(flops=0, bytes_accessed=2 * 1024 * 1024, transcendentals=0),
        name="split_samples",
    )(noise)


def join_samples_kernel(msg_ref, extra_ref, out_ref, tmp_ref):
    rows = msg_ref.shape[1]
    tmp_ref[...] = msg_ref[...].astype(F32).reshape(S * rows, S)
    extra = extra_ref[0]
    for k in range(rows):
        pair = tmp_ref[pl.ds(k, S, stride=rows), :].T
        for yh in range(2):
            column = extra[:, yh * rows + k : yh * rows + k + 1]
            out_ref[yh, k] = pair[yh * BLK : (yh + 1) * BLK] + column


def join_samples(msg, extra):
    rows = 16
    steps = HALF // rows
    cols = extra.reshape(2, steps, rows, BLK).transpose(1, 3, 0, 2).reshape(steps, BLK, 2 * rows)
    out = pl.pallas_call(
        join_samples_kernel,
        grid=(steps,),
        out_shape=jax.ShapeDtypeStruct((2, HALF, BLK, S), F32),
        in_specs=[
            pl.BlockSpec((S, rows, S), lambda i: (0, i, 0)),
            pl.BlockSpec((1, BLK, 2 * rows), lambda i: (i, 0, 0)),
        ],
        out_specs=pl.BlockSpec((2, rows, BLK, S), lambda i: (0, i, 0, 0)),
        scratch_shapes=[VMEM((S * rows, S), F32)],
        compiler_params=pltpu.CompilerParams(vmem_limit_bytes=32 * 1024 * 1024),
        cost_estimate=pl.CostEstimate(flops=0, bytes_accessed=3 * 1024 * 1024, transcendentals=0),
        name="join_samples",
    )(msg, cols)
    return out.reshape(BLK, BLK, S)


def build_band(band_ref, mats_ref):
    band_ref[...] = jnp.zeros_like(band_ref)
    low = low_lanes((BLK, S))
    zero = jnp.zeros((BLK, S), F32)

    def first(b):
        return mats_ref[b, :, 0:S].astype(F32)

    def second(b):
        return mats_ref[b, :, S : 2 * S].astype(F32)

    def put(row, pair, value):
        band_ref[row * BLK : (row + 1) * BLK, pair * S : (pair + 1) * S] = value.astype(BF16)

    for pair in range(BLOCKS // 2):
        even, odd = 2 * pair, 2 * pair + 1
        put(even, pair, jnp.where(low, first(even), first(odd)))
        put(odd, pair, jnp.where(low, second(odd), swap_halves(first(odd))))
        if pair > 0:
            put(even - 1, pair, jnp.where(low, swap_halves(first(even)), zero))
        if odd + 1 < BLOCKS:
            put(odd + 1, pair, jnp.where(low, zero, swap_halves(second(odd + 1))))


def sample_kernel(
    core_ref,
    coeff_ref,
    rows_ref,
    own_ref,
    other_ref,
    xmats_ref,
    ymats_ref,
    weights_ref,
    out_ref,
    xband,
    yband,
    zb,
    fb,
    uf,
    ub,
    fa,
    fc,
    mis,
    cat,
):
    core = core_ref[0]
    low = low_lanes((HALF, S))
    build_band(xband, xmats_ref)
    build_band(yband, ymats_ref)

    @pl.loop(0, 8)
    def _(gc):
        for ref, parity in ((own_ref, core), (other_ref, 1 - core)):
            row = pl.multiple_of((2 * gc + parity) * BLK, BLK)
            for pair in range(BLOCKS // 2):
                a = ref[2 * pair, gc].astype(F32)
                b = ref[2 * pair + 1, gc].astype(F32)
                cols = slice(pair * S, (pair + 1) * S)
                zb[pl.ds(row, HALF), cols] = jnp.where(low, a, swap_halves(b)).astype(BF16)
                zb[pl.ds(row + HALF, HALF), cols] = jnp.where(low, swap_halves(a), b).astype(BF16)

    def reach(t):
        return max(0, t * TILE - S), min(N, (t + 1) * TILE + S)

    def apply(source, source_b, before, target, z_coeff, scale):
        @pl.loop(0, TILES)
        def _(r):
            rows = pl.ds(pl.multiple_of(r * TILE, TILE), TILE)
            for t in range(TILES):
                lo, hi = reach(t)
                cols = slice(t * TILE, (t + 1) * TILE)
                part = jnp.dot(source_b[rows, lo:hi], xband[lo:hi, cols], preferred_element_type=F32)
                value = NUGGET * source[rows, cols].astype(F32) + part
                uf[rows, cols] = value
                ub[rows, cols] = value.astype(BF16)

        @pl.loop(0, TILES)
        def _(c):
            cols = pl.ds(pl.multiple_of(c * TILE, TILE), TILE)
            for t in range(TILES):
                lo, hi = reach(t)
                rows = slice(t * TILE, (t + 1) * TILE)
                part = jnp.dot(yband[rows, lo:hi], ub[lo:hi, cols], preferred_element_type=F32)
                value = NUGGET * uf[rows, cols] + part
                value = scale * value + z_coeff * zb[rows, cols].astype(F32)
                if before is not None:
                    value = value - before[rows, cols]
                target[rows, cols] = value
                fb[rows, cols] = value.astype(BF16)

    c = [coeff_ref[i] for i in range(6)]
    apply(zb, zb, None, fa, c[4], 2.0 * c[5])
    apply(fa, fb, None, fc, c[3] - c[5], 2.0)
    apply(fc, fb, fa, fa, c[2], 2.0)
    apply(fa, fb, fc, fc, c[1], 2.0)
    apply(fc, fb, fa, fa, c[0], 1.0)

    @pl.loop(0, S, unroll=8)
    def _(r):
        mis[pl.ds(r, 1), :] = fa[pl.ds(rows_ref[r], 1), :]

    high = mis[...].astype(BF16)
    cat[0:S, :] = high
    cat[S : 2 * S, :] = high
    cat[2 * S : 3 * S, :] = (mis[...] - high.astype(F32)).astype(BF16)

    @pl.loop(0, 8)
    def _(gc):
        row = pl.multiple_of((2 * gc + core) * BLK, BLK)
        part = jnp.dot(weights_ref[gc], cat[...], preferred_element_type=F32)
        for pair in range(BLOCKS // 2):
            cols = slice(pair * S, (pair + 1) * S)
            a = fa[pl.ds(row, HALF), cols] - part[0:HALF, cols]
            b = fa[pl.ds(row + HALF, HALF), cols] - part[HALF:BLK, cols]
            out_ref[2 * pair, gc] = jnp.where(low, a, swap_halves(b)).astype(BF16)
            out_ref[2 * pair + 1, gc] = jnp.where(low, swap_halves(a), b).astype(BF16)


def sample_all(core, coeff, rows, own, other, xmats, ymats, weights):
    smem = pl.BlockSpec(memory_space=SMEM)
    vmem = pl.BlockSpec(memory_space=VMEM)
    return pl.pallas_call(
        sample_kernel,
        out_shape=jax.ShapeDtypeStruct((16, 8, HALF, S), BF16),
        in_specs=[smem, smem, smem, vmem, vmem, vmem, vmem, vmem],
        out_specs=vmem,
        scratch_shapes=[
            VMEM((N, N), BF16),
            VMEM((N, N), BF16),
            VMEM((N, N), BF16),
            VMEM((N, N), BF16),
            VMEM((N, N), F32),
            VMEM((N, N), BF16),
            VMEM((N, N), F32),
            VMEM((N, N), F32),
            VMEM((S, N), F32),
            VMEM((3 * S, N), BF16),
        ],
        compiler_params=pltpu.CompilerParams(vmem_limit_bytes=48 * 1024 * 1024),
        cost_estimate=pl.CostEstimate(
            flops=10 * 2 * N * N * 512, bytes_accessed=5 * 1024 * 1024, transcendentals=0
        ),
        name="sample_all",
    )(core, coeff, rows, own, other, xmats, ymats, weights)


def body(noise, cheb_coeff, diag_x, couple_x, diag_y, couple_y, track_rows, track_obs, weights):
    core = lax.axis_index("core")
    block = lax.axis_index("gc") * 2 + core
    gy = ("gc", "core")
    chips = ("gx", "gc")

    kx = couple_x.astype(F32)
    empty = jnp.zeros((BLK, BLK), F32)
    xpay = jnp.concatenate([diag_x.T, kx.T, kx, empty], axis=1)
    xmats = lax.all_gather(xpay, "gx", axis=0, tiled=False).astype(BF16)

    ky = couple_y
    local = (track_rows - block * BLK).astype(BF16)
    marks = jnp.zeros((BLK, BLK), BF16).at[0:8, 0].set(local)
    w_high = weights.astype(BF16)
    w_low = (weights - w_high.astype(F32)).astype(BF16)
    ypay = jnp.concatenate([diag_y.astype(BF16), ky.T, ky, marks, w_high, w_low], axis=1)
    ymats = lax.all_gather(ypay, gy, axis=0, tiled=False)
    rows = ymats[:, 0:8, 3 * BLK].astype(jnp.int32) + BLK * jnp.arange(16, dtype=jnp.int32)[:, None]
    own_w = lax.dynamic_index_in_dim(
        ymats[:, :, 4 * BLK :].reshape(8, 2, BLK, 2 * S), core, axis=1, keepdims=False
    )
    own_w = jnp.concatenate([own_w, own_w[:, :, 0:S]], axis=2)

    sent = split_samples(noise)
    own = lax.all_to_all(sent, chips, 0, 0, tiled=True)
    other = lax.ppermute(own, "core", [(0, 1), (1, 0)])
    shape = (16, 8, HALF, S)
    result = sample_all(
        core.reshape(1).astype(jnp.int32),
        cheb_coeff,
        rows.reshape(S),
        own.reshape(shape),
        other.reshape(shape),
        xmats,
        ymats[:, :, 0 : 4 * BLK],
        own_w,
    )
    back = lax.all_to_all(result.reshape(S, HALF, S), chips, 0, 0, tiled=True)

    obs = lax.all_gather(track_obs, gy, axis=0, tiled=True)
    extra = jnp.dot(weights, obs, precision=lax.Precision.HIGHEST, preferred_element_type=F32)
    return join_samples(back, extra)


def solution(mesh):
    fine = Mesh(mesh.devices.reshape(16, 8, 2), ("gx", "gc", "core"))
    rows = ("gc", "core")
    return jax.shard_map(
        body,
        mesh=fine,
        in_specs=(
            P(rows, "gx", None),
            P(),
            P("gx", None),
            P("gx", None),
            P(rows, None),
            P(rows, None),
            P(rows),
            P(rows, "gx"),
            P(rows, None),
        ),
        out_specs=P(rows, "gx", None),
        check_vma=False,
    )
```

```python
import functools

import jax
import jax.numpy as jnp
from jax import lax
from jax.experimental import pallas as pl
from jax.experimental.pallas import tpu as pltpu
from jax.sharding import Mesh, PartitionSpec as P

NUGGET = 0.3
BLK = 64
HALF = 32
N = 1024
S = 128
TILE = 256
TILES = N // TILE
BLOCKS = N // BLK
F32 = jnp.float32
BF16 = jnp.bfloat16
VMEM = pltpu.VMEM
SMEM = pltpu.SMEM


def low_lanes(shape):
    return lax.broadcasted_iota(jnp.int32, shape, len(shape) - 1) < BLK


def swap_halves(value):
    return pltpu.roll(value, BLK, axis=1)


def split_samples_kernel(noise_ref, out_ref, tmp_ref):
    for k in range(HALF):
        pair = jnp.concatenate([noise_ref[k], noise_ref[HALF + k]], axis=0).astype(F32)
        tmp_ref[pl.ds(k, S, stride=HALF), :] = pair.T
    out_ref[...] = tmp_ref[...].reshape(S, HALF, S).astype(BF16)


def split_samples(noise):
    return pl.pallas_call(
        split_samples_kernel,
        out_shape=jax.ShapeDtypeStruct((S, HALF, S), BF16),
        in_specs=[pl.BlockSpec(memory_space=VMEM)],
        out_specs=pl.BlockSpec(memory_space=VMEM),
        scratch_shapes=[VMEM((S * HALF, S), F32)],
        compiler_params=pltpu.CompilerParams(vmem_limit_bytes=32 * 1024 * 1024),
        cost_estimate=pl.CostEstimate(flops=0, bytes_accessed=2 * 1024 * 1024, transcendentals=0),
        name="split_samples",
    )(noise)


def join_samples_kernel(msg_ref, extra_ref, out_ref, tmp_ref):
    rows = msg_ref.shape[1]
    tmp_ref[...] = msg_ref[...].astype(F32).reshape(S * rows, S)
    extra = extra_ref[0]
    for k in range(rows):
        pair = tmp_ref[pl.ds(k, S, stride=rows), :].T
        for yh in range(2):
            column = extra[:, yh * rows + k : yh * rows + k + 1]
            out_ref[yh, k] = pair[yh * BLK : (yh + 1) * BLK] + column


def join_samples(msg, extra):
    rows = 16
    steps = HALF // rows
    cols = extra.reshape(2, steps, rows, BLK).transpose(1, 3, 0, 2).reshape(steps, BLK, 2 * rows)
    out = pl.pallas_call(
        join_samples_kernel,
        grid=(steps,),
        out_shape=jax.ShapeDtypeStruct((2, HALF, BLK, S), F32),
        in_specs=[
            pl.BlockSpec((S, rows, S), lambda i: (0, i, 0)),
            pl.BlockSpec((1, BLK, 2 * rows), lambda i: (i, 0, 0)),
        ],
        out_specs=pl.BlockSpec((2, rows, BLK, S), lambda i: (0, i, 0, 0)),
        scratch_shapes=[VMEM((S * rows, S), F32)],
        compiler_params=pltpu.CompilerParams(vmem_limit_bytes=32 * 1024 * 1024),
        cost_estimate=pl.CostEstimate(flops=0, bytes_accessed=3 * 1024 * 1024, transcendentals=0),
        name="join_samples",
    )(msg, cols)
    return out.reshape(BLK, BLK, S)


def payload_kernel(
    block_ref, track_ref, dx_ref, kx_ref, dy_ref, ky_ref, weights_ref, obs_ref, x_ref, y_ref
):
    x_ref[...] = jnp.concatenate([dx_ref[...].T, kx_ref[...].astype(F32)], axis=1).astype(BF16)
    y_ref[:, 0:S] = jnp.concatenate([dy_ref[...], ky_ref[...].astype(F32)], axis=1).astype(BF16)
    weights = weights_ref[...]
    high = weights.astype(BF16)
    y_ref[:, S : 2 * S] = high
    y_ref[:, 2 * S : 3 * S] = (weights - high.astype(F32)).astype(BF16)
    obs = obs_ref[...]
    one = obs.astype(BF16).astype(F32)
    two = (obs - one).astype(BF16).astype(F32)
    three = obs - one - two
    row = lax.broadcasted_iota(jnp.int32, (8, BLK), 0)
    local = jnp.zeros((8, BLK), F32)
    for j in range(8):
        local = jnp.where(row == j, (track_ref[j] - block_ref[0] * BLK).astype(F32), local)
    extra = jnp.concatenate(
        [
            jnp.concatenate([one, two], axis=1),
            jnp.concatenate([three, local], axis=1),
            jnp.zeros((BLK - 16, S), F32),
        ],
        axis=0,
    )
    y_ref[:, 3 * S : 4 * S] = extra.astype(BF16)


def payloads(block, tracks, dx, kx, dy, ky, weights, obs):
    smem = pl.BlockSpec(memory_space=SMEM)
    vmem = pl.BlockSpec(memory_space=VMEM)
    return pl.pallas_call(
        payload_kernel,
        out_shape=(
            jax.ShapeDtypeStruct((BLK, S), BF16),
            jax.ShapeDtypeStruct((BLK, 4 * S), BF16),
        ),
        in_specs=[smem, smem] + [vmem] * 6,
        out_specs=(vmem, vmem),
        name="payloads",
    )(block, tracks, dx, kx, dy, ky, weights, obs)


def reach(t):
    return max(0, t * TILE - S), min(N, (t + 1) * TILE + S)


def base(t):
    return t * TILE - S


def band_kernel(transposed, place_ref, mats_ref, t_ref, e_ref, dense):
    dense[...] = jnp.zeros_like(dense)
    zero = jnp.zeros((BLK, BLK), F32)

    def put(row, pair, left, right):
        dense[row * BLK : (row + 1) * BLK, pair * S : (pair + 1) * S] = jnp.concatenate(
            [left, right], axis=1
        ).astype(BF16)

    def block(b):
        both = mats_ref[place_ref[b], :, 0:S].astype(F32)
        return both[:, 0:BLK], both[:, BLK:S], both.T[BLK:S, :]

    for pair in range(BLOCKS // 2):
        even, odd = 2 * pair, 2 * pair + 1
        d_even, k_even, back_even = block(even)
        d_odd, k_odd, back_odd = block(odd)
        put(even, pair, d_even, back_odd)
        put(odd, pair, k_odd, d_odd)
        if pair > 0:
            put(even - 1, pair, back_even, zero)
            put(even, pair - 1, zero, k_even)

    for t in range(TILES):
        lo, hi = reach(t)
        mine = slice(t * TILE, (t + 1) * TILE)
        near = slice(lo - base(t), hi - base(t))
        if transposed:
            one = dense[lo:hi, mine]
            two = jnp.dot(dense[lo:hi, lo:hi], one, preferred_element_type=F32)
        else:
            one = dense[mine, lo:hi]
            two = jnp.dot(one, dense[lo:hi, lo:hi], preferred_element_type=F32)
        two = ((2.0 * NUGGET) * one.astype(F32) + two).astype(BF16)
        if transposed:
            t_ref[t, near, :] = one
            e_ref[t, near, :] = two
        else:
            t_ref[t, :, near] = one
            e_ref[t, :, near] = two


def bands(place, mats, transposed):
    shape = (TILES, 2 * TILE, TILE) if transposed else (TILES, TILE, 2 * TILE)
    vmem = pl.BlockSpec(memory_space=VMEM)
    return pl.pallas_call(
        functools.partial(band_kernel, transposed),
        out_shape=(jax.ShapeDtypeStruct(shape, BF16),) * 2,
        in_specs=[pl.BlockSpec(memory_space=SMEM), vmem],
        out_specs=(vmem, vmem),
        scratch_shapes=[VMEM((N, N), BF16)],
        compiler_params=pltpu.CompilerParams(vmem_limit_bytes=24 * 1024 * 1024),
        cost_estimate=pl.CostEstimate(
            flops=2 * 4 * TILE * TILE * 4 * TILE, bytes_accessed=3 * 1024 * 1024, transcendentals=0
        ),
        name="x_bands" if transposed else "y_bands",
    )(place, mats)


def sample_kernel(
    core_ref,
    coeff_ref,
    rows_ref,
    own_ref,
    other_ref,
    xt_ref,
    xe_ref,
    yt_ref,
    ye_ref,
    ymats_ref,
    out_ref,
    zb,
    fb,
    uf,
    ub,
    fa,
    fc,
    mis,
    cat,
    wcat,
):
    core = core_ref[0]
    low = low_lanes((HALF, S))

    @pl.loop(0, 8)
    def _(gc):
        for ref, parity in ((own_ref, core), (other_ref, 1 - core)):
            row = pl.multiple_of((2 * gc + parity) * BLK, BLK)
            for pair in range(BLOCKS // 2):
                a = ref[2 * pair, gc].astype(F32)
                b = ref[2 * pair + 1, gc].astype(F32)
                cols = slice(pair * S, (pair + 1) * S)
                zb[pl.ds(row, HALF), cols] = jnp.where(low, a, swap_halves(b)).astype(BF16)
                zb[pl.ds(row + HALF, HALF), cols] = jnp.where(low, swap_halves(a), b).astype(BF16)

    def along_x(source, source_b, band, share):
        for t in range(TILES):
            lo, hi = reach(t)
            cols = slice(t * TILE, (t + 1) * TILE)
            matrix = band[t, lo - base(t) : hi - base(t), :]
            part = jnp.dot(source_b[:, lo:hi], matrix, preferred_element_type=F32)
            value = share * source[:, cols].astype(F32) + part
            uf[:, cols] = value
            ub[:, cols] = value.astype(BF16)

    def along_y(band, share, finish):
        for t in range(TILES):
            lo, hi = reach(t)
            rows = slice(t * TILE, (t + 1) * TILE)
            matrix = band[t, :, lo - base(t) : hi - base(t)]
            part = jnp.dot(matrix, ub[lo:hi, :], preferred_element_type=F32)
            finish(rows, share * uf[rows, :] + part)

    c = [coeff_ref[i] for i in range(6)]
    square = NUGGET * NUGGET

    def first(rows, value):
        value = 2.0 * value - zb[rows, :].astype(F32)
        fa[rows, :] = value
        fb[rows, :] = value.astype(BF16)

    def second(rows, value):
        once = fa[rows, :]
        start = zb[rows, :].astype(F32)
        twice = 2.0 * value - once
        fa[rows, :] = (c[0] - c[4]) * start + c[2] * once + (2.0 * c[4]) * twice
        odd = (c[1] - c[3] - c[5]) * start + (2.0 * (c[3] - c[5])) * once + (4.0 * c[5]) * twice
        fc[rows, :] = odd
        fb[rows, :] = odd.astype(BF16)

    def third(rows, value):
        fa[rows, :] = fa[rows, :] + value

    along_x(zb, zb, xe_ref, square)
    along_y(ye_ref, square, first)
    along_x(fa, fb, xe_ref, square)
    along_y(ye_ref, square, second)
    along_x(fc, fb, xt_ref, NUGGET)
    along_y(yt_ref, NUGGET, third)

    @pl.loop(0, S, unroll=8)
    def _(r):
        mis[pl.ds(r, 1), :] = fa[pl.ds(rows_ref[r], 1), :]

    high = mis[...].astype(BF16)
    cat[0:S, :] = high
    cat[S : 2 * S, :] = high
    cat[2 * S : 3 * S, :] = (mis[...] - high.astype(F32)).astype(BF16)
    for gc in range(8):
        w = ymats_ref[2 * gc + core, :, S : 3 * S]
        wcat[gc * BLK : (gc + 1) * BLK, 0 : 2 * S] = w
        wcat[gc * BLK : (gc + 1) * BLK, 2 * S : 3 * S] = w[:, 0:S]
    uf[0 : 8 * BLK, :] = jnp.dot(wcat[...], cat[...], preferred_element_type=F32)

    @pl.loop(0, 8)
    def _(gc):
        row = pl.multiple_of((2 * gc + core) * BLK, BLK)
        mine = pl.multiple_of(gc * BLK, BLK)
        for pair in range(BLOCKS // 2):
            cols = slice(pair * S, (pair + 1) * S)
            a = fa[pl.ds(row, HALF), cols] - uf[pl.ds(mine, HALF), cols]
            b = fa[pl.ds(row + HALF, HALF), cols] - uf[pl.ds(mine + HALF, HALF), cols]
            out_ref[2 * pair, gc] = jnp.where(low, a, swap_halves(b)).astype(BF16)
            out_ref[2 * pair + 1, gc] = jnp.where(low, swap_halves(a), b).astype(BF16)


def sample_all(core, coeff, rows, own, other, xt, xe, yt, ye, ymats):
    smem = pl.BlockSpec(memory_space=SMEM)
    vmem = pl.BlockSpec(memory_space=VMEM)
    return pl.pallas_call(
        sample_kernel,
        out_shape=jax.ShapeDtypeStruct((16, 8, HALF, S), BF16),
        in_specs=[smem, smem, smem] + [vmem] * 7,
        out_specs=vmem,
        scratch_shapes=[
            VMEM((N, N), BF16),
            VMEM((N, N), BF16),
            VMEM((N, N), F32),
            VMEM((N, N), BF16),
            VMEM((N, N), F32),
            VMEM((N, N), F32),
            VMEM((S, N), F32),
            VMEM((3 * S, N), BF16),
            VMEM((8 * BLK, 3 * S), BF16),
        ],
        compiler_params=pltpu.CompilerParams(vmem_limit_bytes=44 * 1024 * 1024),
        cost_estimate=pl.CostEstimate(
            flops=6 * 2 * N * N * 512, bytes_accessed=5 * 1024 * 1024, transcendentals=0
        ),
        name="sample_all",
    )(core, coeff, rows, own, other, xt, xe, yt, ye, ymats)


def gather_ring(value, axis):
    size = lax.axis_size(axis)
    parts = [value] + [
        lax.ppermute(value, axis, [(i, (i + step) % size) for i in range(size)])
        for step in range(1, size)
    ]
    return jnp.stack(parts)


def body(noise, cheb_coeff, diag_x, couple_x, diag_y, couple_y, track_rows, track_obs, weights):
    core = lax.axis_index("core")
    block = lax.axis_index("gc") * 2 + core
    gy = ("gc", "core")
    chips = ("zh", "x", "gc")

    xpay, ypay = payloads(
        block.reshape(1).astype(jnp.int32),
        track_rows,
        diag_x,
        couple_x,
        diag_y,
        couple_y,
        weights,
        track_obs,
    )
    noise, xpay, ypay = lax.optimization_barrier((noise, xpay, ypay))
    ymats = lax.all_gather(ypay, gy, axis=0, tiled=False)
    sent = split_samples(noise)
    own = lax.all_to_all(sent, chips, 0, 0, tiled=True)

    xmats = gather_ring(gather_ring(xpay, "x"), "zh").reshape(16, BLK, S)
    index = jnp.arange(16, dtype=jnp.int32)
    far = (lax.axis_index("zh") - index // 4) % 4
    near = (lax.axis_index("x") - index % 4) % 4
    xt, xe = bands(far * 4 + near, xmats, True)
    yt, ye = bands(index, ymats, False)
    rows = ymats[:, 8:16, 3 * S + BLK].astype(jnp.int32) + BLK * index[:, None]
    rows = rows.reshape(S)
    own, xt, xe, yt, ye, rows = lax.optimization_barrier((own, xt, xe, yt, ye, rows))

    other = lax.ppermute(own, "core", [(0, 1), (1, 0)])
    shape = (16, 8, HALF, S)
    result = sample_all(
        core.reshape(1).astype(jnp.int32),
        cheb_coeff,
        rows,
        own.reshape(shape),
        other.reshape(shape),
        xt,
        xe,
        yt,
        ye,
        ymats,
    )
    back = lax.all_to_all(result.reshape(S, HALF, S), chips, 0, 0, tiled=True)

    parts = ymats[:, 0:16, 3 * S : 4 * S].astype(F32)
    obs = parts[:, 0:8, 0:BLK] + parts[:, 0:8, BLK:S] + parts[:, 8:16, 0:BLK]
    extra = jnp.dot(
        weights,
        obs.reshape(S, BLK),
        precision=lax.Precision.HIGHEST,
        preferred_element_type=F32,
    )
    return join_samples(back, extra)


def solution(mesh):
    fine = Mesh(mesh.devices.reshape(4, 4, 8, 2), ("zh", "x", "gc", "core"))
    rows = ("gc", "core")
    cols = ("zh", "x")
    return jax.shard_map(
        body,
        mesh=fine,
        in_specs=(
            P(rows, cols, None),
            P(),
            P(cols, None),
            P(cols, None),
            P(rows, None),
            P(rows, None),
            P(rows),
            P(rows, cols),
            P(rows, None),
        ),
        out_specs=P(rows, cols, None),
        check_vma=False,
    )
```

```python
import functools

import jax
import jax.numpy as jnp
from jax import lax
from jax.experimental import pallas as pl
from jax.experimental.pallas import tpu as pltpu
from jax.sharding import Mesh, PartitionSpec as P

NUGGET = 0.3
BLK = 64
HALF = 32
N = 1024
S = 128
TILE = 256
TILES = N // TILE
BLOCKS = N // BLK
F32 = jnp.float32
BF16 = jnp.bfloat16
VMEM = pltpu.VMEM
SMEM = pltpu.SMEM


def low_lanes(shape):
    return lax.broadcasted_iota(jnp.int32, shape, len(shape) - 1) < BLK


def swap_halves(value):
    return pltpu.roll(value, BLK, axis=1)


def split_samples_kernel(noise_ref, out_ref, tmp_ref):
    rows = out_ref.shape[1]
    for k in range(rows):
        pair = jnp.concatenate([noise_ref[0, k], noise_ref[1, k]], axis=0).astype(F32)
        tmp_ref[pl.ds(k, S, stride=rows), :] = pair.T
    out_ref[...] = tmp_ref[...].reshape(S, rows, S).astype(BF16)


def split_samples(noise):
    rows = 16
    return pl.pallas_call(
        split_samples_kernel,
        grid=(HALF // rows,),
        out_shape=jax.ShapeDtypeStruct((S, HALF, S), BF16),
        in_specs=[pl.BlockSpec((2, rows, BLK, S), lambda i: (0, i, 0, 0))],
        out_specs=pl.BlockSpec((S, rows, S), lambda i: (0, i, 0)),
        scratch_shapes=[VMEM((S * rows, S), F32)],
        compiler_params=pltpu.CompilerParams(vmem_limit_bytes=16 * 1024 * 1024),
        cost_estimate=pl.CostEstimate(flops=0, bytes_accessed=2 * 1024 * 1024, transcendentals=0),
        name="split_samples",
    )(noise.reshape(2, HALF, BLK, S))


def join_samples_kernel(msg_ref, extra_ref, out_ref, tmp_ref):
    rows = msg_ref.shape[1]
    tmp_ref[...] = msg_ref[...].astype(F32).reshape(S * rows, S)
    extra = extra_ref[0]
    for k in range(rows):
        pair = tmp_ref[pl.ds(k, S, stride=rows), :].T
        for yh in range(2):
            column = extra[:, yh * rows + k : yh * rows + k + 1]
            out_ref[yh, k] = pair[yh * BLK : (yh + 1) * BLK] + column


def join_samples(msg, extra):
    rows = 16
    steps = HALF // rows
    cols = extra.reshape(2, steps, rows, BLK).transpose(1, 3, 0, 2).reshape(steps, BLK, 2 * rows)
    out = pl.pallas_call(
        join_samples_kernel,
        grid=(steps,),
        out_shape=jax.ShapeDtypeStruct((2, HALF, BLK, S), F32),
        in_specs=[
            pl.BlockSpec((S, rows, S), lambda i: (0, i, 0)),
            pl.BlockSpec((1, BLK, 2 * rows), lambda i: (i, 0, 0)),
        ],
        out_specs=pl.BlockSpec((2, rows, BLK, S), lambda i: (0, i, 0, 0)),
        scratch_shapes=[VMEM((S * rows, S), F32)],
        compiler_params=pltpu.CompilerParams(vmem_limit_bytes=16 * 1024 * 1024),
        cost_estimate=pl.CostEstimate(flops=0, bytes_accessed=3 * 1024 * 1024, transcendentals=0),
        name="join_samples",
    )(msg, cols)
    return out.reshape(BLK, BLK, S)


def payload_kernel(
    block_ref, track_ref, dx_ref, kx_ref, dy_ref, ky_ref, weights_ref, obs_ref, x_ref, y_ref
):
    x_ref[...] = jnp.concatenate([dx_ref[...].T, kx_ref[...].astype(F32)], axis=1).astype(BF16)
    y_ref[:, 0:S] = jnp.concatenate([dy_ref[...], ky_ref[...].astype(F32)], axis=1).astype(BF16)
    weights = weights_ref[...]
    high = weights.astype(BF16)
    y_ref[:, S : 2 * S] = high
    y_ref[:, 2 * S : 3 * S] = (weights - high.astype(F32)).astype(BF16)
    obs = obs_ref[...]
    one = obs.astype(BF16).astype(F32)
    two = (obs - one).astype(BF16).astype(F32)
    three = obs - one - two
    row = lax.broadcasted_iota(jnp.int32, (8, BLK), 0)
    local = jnp.zeros((8, BLK), F32)
    for j in range(8):
        local = jnp.where(row == j, (track_ref[j] - block_ref[0] * BLK).astype(F32), local)
    extra = jnp.concatenate(
        [
            jnp.concatenate([one, two], axis=1),
            jnp.concatenate([three, local], axis=1),
            jnp.zeros((BLK - 16, S), F32),
        ],
        axis=0,
    )
    y_ref[:, 3 * S : 4 * S] = extra.astype(BF16)


def payloads(block, tracks, dx, kx, dy, ky, weights, obs):
    smem = pl.BlockSpec(memory_space=SMEM)
    vmem = pl.BlockSpec(memory_space=VMEM)
    return pl.pallas_call(
        payload_kernel,
        out_shape=(
            jax.ShapeDtypeStruct((BLK, S), BF16),
            jax.ShapeDtypeStruct((BLK, 4 * S), BF16),
        ),
        in_specs=[smem, smem] + [vmem] * 6,
        out_specs=(vmem, vmem),
        name="payloads",
    )(block, tracks, dx, kx, dy, ky, weights, obs)


def reach(t):
    return max(0, t * TILE - S), min(N, (t + 1) * TILE + S)


def base(t):
    return t * TILE - S


def band_kernel(transposed, place_ref, mine_ref, theirs_ref, t_ref, e_ref, dense):
    dense[...] = jnp.zeros_like(dense)
    zero = jnp.zeros((BLK, BLK), F32)

    def put(row, pair, left, right):
        dense[row * BLK : (row + 1) * BLK, pair * S : (pair + 1) * S] = jnp.concatenate(
            [left, right], axis=1
        ).astype(BF16)

    def block(b):
        if transposed:
            both = mine_ref[place_ref[b], :, 0:S]
        else:
            spot = place_ref[b // 2]
            own = mine_ref[spot, :, 0:S].astype(F32)
            other = theirs_ref[spot, :, 0:S].astype(F32)
            both = jnp.where(place_ref[8] == b % 2, own, other)
        both = both.astype(F32)
        return both[:, 0:BLK], both[:, BLK:S], both.T[BLK:S, :]

    for pair in range(BLOCKS // 2):
        even, odd = 2 * pair, 2 * pair + 1
        d_even, k_even, back_even = block(even)
        d_odd, k_odd, back_odd = block(odd)
        put(even, pair, d_even, back_odd)
        put(odd, pair, k_odd, d_odd)
        if pair > 0:
            put(even - 1, pair, back_even, zero)
            put(even, pair - 1, zero, k_even)

    for t in range(TILES):
        lo, hi = reach(t)
        mine = slice(t * TILE, (t + 1) * TILE)
        near = slice(lo - base(t), hi - base(t))
        if transposed:
            one = dense[lo:hi, mine]
            two = jnp.dot(dense[lo:hi, lo:hi], one, preferred_element_type=F32)
        else:
            one = dense[mine, lo:hi]
            two = jnp.dot(one, dense[lo:hi, lo:hi], preferred_element_type=F32)
        two = ((2.0 * NUGGET) * one.astype(F32) + two).astype(BF16)
        if transposed:
            t_ref[t, near, :] = one
            e_ref[t, near, :] = two
        else:
            t_ref[t, :, near] = one
            e_ref[t, :, near] = two


def bands(place, mine, theirs, transposed):
    shape = (TILES, 2 * TILE, TILE) if transposed else (TILES, TILE, 2 * TILE)
    vmem = pl.BlockSpec(memory_space=VMEM)
    return pl.pallas_call(
        functools.partial(band_kernel, transposed),
        out_shape=(jax.ShapeDtypeStruct(shape, BF16),) * 2,
        in_specs=[pl.BlockSpec(memory_space=SMEM), vmem, vmem],
        out_specs=(vmem, vmem),
        scratch_shapes=[VMEM((N, N), BF16)],
        compiler_params=pltpu.CompilerParams(vmem_limit_bytes=12 * 1024 * 1024),
        cost_estimate=pl.CostEstimate(
            flops=2 * 4 * TILE * TILE * 4 * TILE, bytes_accessed=3 * 1024 * 1024, transcendentals=0
        ),
        name="x_bands" if transposed else "y_bands",
    )(place, mine, theirs)


def sample_kernel(
    place_ref,
    coeff_ref,
    rows_ref,
    own_ref,
    other_ref,
    xt_ref,
    xe_ref,
    yt_ref,
    ye_ref,
    ymine_ref,
    out_ref,
    zb,
    fb,
    uf,
    ub,
    fa,
    fc,
    mis,
    cat,
    wcat,
):
    core = place_ref[8]
    low = low_lanes((HALF, S))

    @pl.loop(0, 8)
    def _(gc):
        for ref, parity in ((own_ref, core), (other_ref, 1 - core)):
            row = pl.multiple_of((2 * gc + parity) * BLK, BLK)
            for pair in range(BLOCKS // 2):
                a = ref[2 * pair, gc].astype(F32)
                b = ref[2 * pair + 1, gc].astype(F32)
                cols = slice(pair * S, (pair + 1) * S)
                zb[pl.ds(row, HALF), cols] = jnp.where(low, a, swap_halves(b)).astype(BF16)
                zb[pl.ds(row + HALF, HALF), cols] = jnp.where(low, swap_halves(a), b).astype(BF16)

    def along_x(source, source_b, band, share):
        for t in range(TILES):
            lo, hi = reach(t)
            cols = slice(t * TILE, (t + 1) * TILE)
            matrix = band[t, lo - base(t) : hi - base(t), :]
            part = jnp.dot(source_b[:, lo:hi], matrix, preferred_element_type=F32)
            value = share * source[:, cols].astype(F32) + part
            uf[:, cols] = value
            ub[:, cols] = value.astype(BF16)

    def along_y(band, share, finish):
        for t in range(TILES):
            lo, hi = reach(t)
            rows = slice(t * TILE, (t + 1) * TILE)
            matrix = band[t, :, lo - base(t) : hi - base(t)]
            part = jnp.dot(matrix, ub[lo:hi, :], preferred_element_type=F32)
            finish(rows, share * uf[rows, :] + part)

    c = [coeff_ref[i] for i in range(6)]
    square = NUGGET * NUGGET

    def first(rows, value):
        value = 2.0 * value - zb[rows, :].astype(F32)
        fa[rows, :] = value
        fb[rows, :] = value.astype(BF16)

    def second(rows, value):
        once = fa[rows, :]
        start = zb[rows, :].astype(F32)
        twice = 2.0 * value - once
        fa[rows, :] = (c[0] - c[4]) * start + c[2] * once + (2.0 * c[4]) * twice
        odd = (c[1] - c[3] - c[5]) * start + (2.0 * (c[3] - c[5])) * once + (4.0 * c[5]) * twice
        fc[rows, :] = odd
        fb[rows, :] = odd.astype(BF16)

    def third(rows, value):
        fa[rows, :] = fa[rows, :] + value

    along_x(zb, zb, xe_ref, square)
    along_y(ye_ref, square, first)
    along_x(fa, fb, xe_ref, square)
    along_y(ye_ref, square, second)
    along_x(fc, fb, xt_ref, NUGGET)
    along_y(yt_ref, NUGGET, third)

    @pl.loop(0, BLOCKS)
    def _(b):
        side = jnp.where(b % 2 == core, 0, S // 2)
        for j in range(8):
            row = b * BLK + rows_ref[side + place_ref[b // 2] * 8 + j]
            mis[pl.ds(b * 8 + j, 1), :] = fa[pl.ds(row, 1), :]

    high = mis[...].astype(BF16)
    cat[0:S, :] = high
    cat[S : 2 * S, :] = high
    cat[2 * S : 3 * S, :] = (mis[...] - high.astype(F32)).astype(BF16)
    for gc in range(8):
        w = ymine_ref[place_ref[gc], :, S : 3 * S]
        wcat[gc * BLK : (gc + 1) * BLK, 0 : 2 * S] = w
        wcat[gc * BLK : (gc + 1) * BLK, 2 * S : 3 * S] = w[:, 0:S]
    uf[0 : 8 * BLK, :] = jnp.dot(wcat[...], cat[...], preferred_element_type=F32)

    @pl.loop(0, 8)
    def _(gc):
        row = pl.multiple_of((2 * gc + core) * BLK, BLK)
        mine = pl.multiple_of(gc * BLK, BLK)
        for pair in range(BLOCKS // 2):
            cols = slice(pair * S, (pair + 1) * S)
            a = fa[pl.ds(row, HALF), cols] - uf[pl.ds(mine, HALF), cols]
            b = fa[pl.ds(row + HALF, HALF), cols] - uf[pl.ds(mine + HALF, HALF), cols]
            out_ref[2 * pair, gc] = jnp.where(low, a, swap_halves(b)).astype(BF16)
            out_ref[2 * pair + 1, gc] = jnp.where(low, swap_halves(a), b).astype(BF16)


def sample_all(place, coeff, rows, own, other, xt, xe, yt, ye, ymine):
    smem = pl.BlockSpec(memory_space=SMEM)
    vmem = pl.BlockSpec(memory_space=VMEM)
    return pl.pallas_call(
        sample_kernel,
        out_shape=jax.ShapeDtypeStruct((16, 8, HALF, S), BF16),
        in_specs=[smem, smem, smem] + [vmem] * 7,
        out_specs=vmem,
        scratch_shapes=[
            VMEM((N, N), BF16),
            VMEM((N, N), BF16),
            VMEM((N, N), F32),
            VMEM((N, N), BF16),
            VMEM((N, N), F32),
            VMEM((N, N), F32),
            VMEM((S, N), F32),
            VMEM((3 * S, N), BF16),
            VMEM((8 * BLK, 3 * S), BF16),
        ],
        compiler_params=pltpu.CompilerParams(vmem_limit_bytes=28 * 1024 * 1024),
        cost_estimate=pl.CostEstimate(
            flops=6 * 2 * N * N * 512, bytes_accessed=5 * 1024 * 1024, transcendentals=0
        ),
        name="sample_all",
    )(place, coeff, rows, own, other, xt, xe, yt, ye, ymine)


def gather_ring(value, axis):
    size = lax.axis_size(axis)
    parts = [value] + [
        lax.ppermute(value, axis, [(i, (i + step) % size) for i in range(size)])
        for step in range(1, size)
    ]
    return jnp.stack(parts)


def body(noise, cheb_coeff, diag_x, couple_x, diag_y, couple_y, track_rows, track_obs, weights):
    core = lax.axis_index("core")
    y = lax.axis_index("y")
    zl = lax.axis_index("zl")
    chips = ("zh", "x", "y", "zl")

    xpay, ypay = payloads(
        (y * 4 + zl * 2 + core).reshape(1).astype(jnp.int32),
        track_rows,
        diag_x,
        couple_x,
        diag_y,
        couple_y,
        weights,
        track_obs,
    )
    xfar = gather_ring(xpay, "zh")
    yfar = gather_ring(ypay, "zl")
    sent = split_samples(noise)
    sent, xfar, yfar = lax.optimization_barrier((sent, xfar, yfar))
    own = lax.all_to_all(sent, chips, 0, 0, tiled=True)

    xmats = gather_ring(xfar, "x").reshape(16, BLK, S)
    ymine = gather_ring(yfar, "y").reshape(8, BLK, 4 * S)
    ytheirs = lax.ppermute(ymine, "core", [(0, 1), (1, 0)])
    own, xmats, ymine, ytheirs = lax.optimization_barrier((own, xmats, ymine, ytheirs))
    other = lax.ppermute(own, "core", [(0, 1), (1, 0)])

    index = jnp.arange(16, dtype=jnp.int32)
    near = (lax.axis_index("x") - index % 4) % 4
    far = (lax.axis_index("zh") - index // 4) % 4
    xt, xe = bands(near * 4 + far, xmats, xmats[0:1], True)
    index = jnp.arange(9, dtype=jnp.int32)
    place = (y - index // 2) % 4 * 2 + (zl - index) % 2
    place = jnp.where(index == 8, core, place).astype(jnp.int32)
    yt, ye = bands(place, ymine, ytheirs, False)
    extras = jnp.stack([ymine, ytheirs])[:, :, 0:16, 3 * S : 4 * S]
    rows = extras[:, :, 8:16, BLK].astype(jnp.int32).reshape(S)

    shape = (16, 8, HALF, S)
    result = sample_all(
        place,
        cheb_coeff,
        rows,
        own.reshape(shape),
        other.reshape(shape),
        xt,
        xe,
        yt,
        ye,
        ymine,
    )
    back = lax.all_to_all(result.reshape(S, HALF, S), chips, 0, 0, tiled=True)

    parts = extras.astype(F32)
    obs = parts[:, :, 0:8, 0:BLK] + parts[:, :, 0:8, BLK:S] + parts[:, :, 8:16, 0:BLK]
    block = jnp.arange(16, dtype=jnp.int32)
    spot = (y - block // 4) % 4 * 2 + (zl - block // 2) % 2
    spot = jnp.where(block % 2 == core, spot, spot + 8)
    order = (spot[:, None] == block[None, :]).astype(F32)
    obs = jnp.dot(order, obs.reshape(16, 8 * BLK), precision=lax.Precision.HIGHEST)
    extra = jnp.dot(
        weights,
        obs.reshape(S, BLK),
        precision=lax.Precision.HIGHEST,
        preferred_element_type=F32,
    )
    return join_samples(back, extra)


def solution(mesh):
    fine = Mesh(mesh.devices.reshape(4, 4, 4, 2, 2), ("zh", "x", "y", "zl", "core"))
    rows = ("y", "zl", "core")
    cols = ("zh", "x")
    return jax.shard_map(
        body,
        mesh=fine,
        in_specs=(
            P(rows, cols, None),
            P(),
            P(cols, None),
            P(cols, None),
            P(rows, None),
            P(rows, None),
            P(rows),
            P(rows, cols),
            P(rows, None),
        ),
        out_specs=P(rows, cols, None),
        check_vma=False,
    )
```

```python
import functools

import jax
import jax.numpy as jnp
from jax import lax
from jax.experimental import pallas as pl
from jax.experimental.pallas import tpu as pltpu
from jax.sharding import Mesh, PartitionSpec as P

NUGGET = 0.3
BLK = 64
HALF = 32
N = 1024
S = 128
TILE = 256
TILES = N // TILE
BLOCKS = N // BLK
F32 = jnp.float32
BF16 = jnp.bfloat16
VMEM = pltpu.VMEM
SMEM = pltpu.SMEM


def low_lanes(shape):
    return lax.broadcasted_iota(jnp.int32, shape, len(shape) - 1) < BLK


def swap_halves(value):
    return pltpu.roll(value, BLK, axis=1)


def split_samples_kernel(noise_ref, out_ref, tmp_ref):
    rows = out_ref.shape[1]
    for k in range(rows):
        pair = jnp.concatenate([noise_ref[0, k], noise_ref[1, k]], axis=0).astype(F32)
        tmp_ref[pl.ds(k, S, stride=rows), :] = pair.T
    out_ref[...] = tmp_ref[...].reshape(S, rows, S).astype(BF16)


def split_samples(noise):
    rows = 16
    return pl.pallas_call(
        split_samples_kernel,
        grid=(HALF // rows,),
        out_shape=jax.ShapeDtypeStruct((S, HALF, S), BF16),
        in_specs=[pl.BlockSpec((2, rows, BLK, S), lambda i: (0, i, 0, 0))],
        out_specs=pl.BlockSpec((S, rows, S), lambda i: (0, i, 0)),
        scratch_shapes=[VMEM((S * rows, S), F32)],
        compiler_params=pltpu.CompilerParams(vmem_limit_bytes=60 * 1024 * 1024),
        cost_estimate=pl.CostEstimate(flops=0, bytes_accessed=2 * 1024 * 1024, transcendentals=0),
        name="split_samples",
    )(noise.reshape(2, HALF, BLK, S))


def join_samples_kernel(msg_ref, extra_ref, out_ref, tmp_ref):
    rows = msg_ref.shape[1]
    tmp_ref[...] = msg_ref[...].astype(F32).reshape(S * rows, S)
    extra = extra_ref[0]
    for k in range(rows):
        pair = tmp_ref[pl.ds(k, S, stride=rows), :].T
        for yh in range(2):
            column = extra[:, yh * rows + k : yh * rows + k + 1]
            out_ref[yh, k] = pair[yh * BLK : (yh + 1) * BLK] + column


def join_samples(msg, extra):
    rows = 16
    steps = HALF // rows
    cols = extra.reshape(2, steps, rows, BLK).transpose(1, 3, 0, 2).reshape(steps, BLK, 2 * rows)
    out = pl.pallas_call(
        join_samples_kernel,
        grid=(steps,),
        out_shape=jax.ShapeDtypeStruct((2, HALF, BLK, S), F32),
        in_specs=[
            pl.BlockSpec((S, rows, S), lambda i: (0, i, 0)),
            pl.BlockSpec((1, BLK, 2 * rows), lambda i: (i, 0, 0)),
        ],
        out_specs=pl.BlockSpec((2, rows, BLK, S), lambda i: (0, i, 0, 0)),
        scratch_shapes=[VMEM((S * rows, S), F32)],
        compiler_params=pltpu.CompilerParams(vmem_limit_bytes=16 * 1024 * 1024),
        cost_estimate=pl.CostEstimate(flops=0, bytes_accessed=3 * 1024 * 1024, transcendentals=0),
        name="join_samples",
    )(msg, cols)
    return out.reshape(BLK, BLK, S)


def payload_kernel(
    block_ref, track_ref, dx_ref, kx_ref, dy_ref, ky_ref, weights_ref, obs_ref, x_ref, y_ref
):
    x_ref[...] = jnp.concatenate([dx_ref[...].T, kx_ref[...].astype(F32)], axis=1).astype(BF16)
    y_ref[:, 0:S] = jnp.concatenate([dy_ref[...], ky_ref[...].astype(F32)], axis=1).astype(BF16)
    weights = weights_ref[...]
    high = weights.astype(BF16)
    y_ref[:, S : 2 * S] = high
    y_ref[:, 2 * S : 3 * S] = (weights - high.astype(F32)).astype(BF16)
    obs = obs_ref[...]
    one = obs.astype(BF16).astype(F32)
    two = (obs - one).astype(BF16).astype(F32)
    three = obs - one - two
    row = lax.broadcasted_iota(jnp.int32, (8, BLK), 0)
    local = jnp.zeros((8, BLK), F32)
    for j in range(8):
        local = jnp.where(row == j, (track_ref[j] - block_ref[0] * BLK).astype(F32), local)
    extra = jnp.concatenate(
        [
            jnp.concatenate([one, two], axis=1),
            jnp.concatenate([three, local], axis=1),
            jnp.zeros((BLK - 16, S), F32),
        ],
        axis=0,
    )
    y_ref[:, 3 * S : 4 * S] = extra.astype(BF16)


def payloads(block, tracks, dx, kx, dy, ky, weights, obs):
    smem = pl.BlockSpec(memory_space=SMEM)
    vmem = pl.BlockSpec(memory_space=VMEM)
    return pl.pallas_call(
        payload_kernel,
        out_shape=(
            jax.ShapeDtypeStruct((BLK, S), BF16),
            jax.ShapeDtypeStruct((BLK, 4 * S), BF16),
        ),
        in_specs=[smem, smem] + [vmem] * 6,
        out_specs=(vmem, vmem),
        name="payloads",
    )(block, tracks, dx, kx, dy, ky, weights, obs)


def reach(t):
    return max(0, t * TILE - S), min(N, (t + 1) * TILE + S)


def base(t):
    return t * TILE - S


def band_kernel(
    place_ref, x_ref, mine_ref, theirs_ref, xt_ref, xe_ref, yt_ref, ye_ref, dense
):
    dense[...] = jnp.zeros_like(dense)
    zero = jnp.zeros((BLK, BLK), F32)

    def put(row, pair, left, right):
        dense[row * BLK : (row + 1) * BLK, pair * S : (pair + 1) * S] = jnp.concatenate(
            [left, right], axis=1
        ).astype(BF16)

    def x_block(b):
        return x_ref[place_ref[16 + b], :, 0:S].astype(F32)

    def y_block(b):
        spot = place_ref[b // 2]
        own = mine_ref[spot, :, 0:S].astype(F32)
        other = theirs_ref[spot, :, 0:S].astype(F32)
        return jnp.where(place_ref[8] == b % 2, own, other)

    def split(both):
        return both[:, 0:BLK], both[:, BLK:S], both.T[BLK:S, :]

    for block, t_ref, e_ref in ((x_block, xt_ref, xe_ref), (y_block, yt_ref, ye_ref)):
        for pair in range(BLOCKS // 2):
            even, odd = 2 * pair, 2 * pair + 1
            d_even, k_even, back_even = split(block(even))
            d_odd, k_odd, back_odd = split(block(odd))
            put(even, pair, d_even, back_odd)
            put(odd, pair, k_odd, d_odd)
            if pair > 0:
                put(even - 1, pair, back_even, zero)
                put(even, pair - 1, zero, k_even)
        for t in range(TILES):
            lo, hi = reach(t)
            near = slice(lo - base(t), hi - base(t))
            one = dense[lo:hi, t * TILE : (t + 1) * TILE]
            two = jnp.dot(dense[lo:hi, lo:hi], one, preferred_element_type=F32)
            t_ref[t, near, :] = one
            e_ref[t, near, :] = ((2.0 * NUGGET) * one.astype(F32) + two).astype(BF16)


def bands(place, xmats, mine, theirs):
    vmem = pl.BlockSpec(memory_space=VMEM)
    return pl.pallas_call(
        band_kernel,
        out_shape=(jax.ShapeDtypeStruct((TILES, 2 * TILE, TILE), BF16),) * 4,
        in_specs=[pl.BlockSpec(memory_space=SMEM), vmem, vmem, vmem],
        out_specs=(vmem,) * 4,
        scratch_shapes=[VMEM((N, N), BF16)],
        compiler_params=pltpu.CompilerParams(vmem_limit_bytes=16 * 1024 * 1024),
        cost_estimate=pl.CostEstimate(
            flops=4 * 4 * TILE * TILE * 4 * TILE, bytes_accessed=6 * 1024 * 1024, transcendentals=0
        ),
        name="bands",
    )(place, xmats, mine, theirs)


def sample_kernel(
    place_ref,
    coeff_ref,
    rows_ref,
    own_ref,
    other_ref,
    xt_ref,
    xe_ref,
    yt_ref,
    ye_ref,
    ymine_ref,
    out_ref,
    zb,
    fb,
    uf,
    ub,
    fa,
    fc,
    mis,
    cat,
    wcat,
):
    core = place_ref[8]
    low = low_lanes((HALF, S))

    @pl.loop(0, 8)
    def _(gc):
        for ref, parity in ((own_ref, core), (other_ref, 1 - core)):
            row = pl.multiple_of((2 * gc + parity) * BLK, BLK)
            for pair in range(BLOCKS // 2):
                a = ref[2 * pair, gc].astype(F32)
                b = ref[2 * pair + 1, gc].astype(F32)
                cols = slice(pair * S, (pair + 1) * S)
                zb[pl.ds(row, HALF), cols] = jnp.where(low, a, swap_halves(b)).astype(BF16)
                zb[pl.ds(row + HALF, HALF), cols] = jnp.where(low, swap_halves(a), b).astype(BF16)

    def along_x(source, source_b, band, share):
        for t in range(TILES):
            lo, hi = reach(t)
            cols = slice(t * TILE, (t + 1) * TILE)
            matrix = band[t, lo - base(t) : hi - base(t), :]
            part = jnp.dot(source_b[:, lo:hi], matrix, preferred_element_type=F32)
            value = share * source[:, cols].astype(F32) + part
            uf[:, cols] = value
            ub[:, cols] = value.astype(BF16)

    def along_y(band, share, finish):
        for k in range(TILES):
            lo, hi = reach(k)
            matrix = band[k, lo - base(k) : hi - base(k), :]
            part = jnp.dot(matrix, ub[k * TILE : (k + 1) * TILE, :], preferred_element_type=F32)
            for j in range(lo // S, hi // S):
                rows = slice(j * S, (j + 1) * S)
                value = part[j * S - lo : (j + 1) * S - lo]
                if k == max(0, (j - 1) // 2):
                    value = share * uf[rows, :] + value
                else:
                    value = uf[rows, :] + value
                if k == min(TILES - 1, (j + 1) // 2):
                    finish(rows, value)
                else:
                    uf[rows, :] = value

    c = [coeff_ref[i] for i in range(6)]
    square = NUGGET * NUGGET

    def first(rows, value):
        value = 2.0 * value - zb[rows, :].astype(F32)
        fa[rows, :] = value
        fb[rows, :] = value.astype(BF16)

    def second(rows, value):
        once = fa[rows, :]
        start = zb[rows, :].astype(F32)
        twice = 2.0 * value - once
        fa[rows, :] = (c[0] - c[4]) * start + c[2] * once + (2.0 * c[4]) * twice
        odd = (c[1] - c[3] - c[5]) * start + (2.0 * (c[3] - c[5])) * once + (4.0 * c[5]) * twice
        fc[rows, :] = odd
        fb[rows, :] = odd.astype(BF16)

    def third(rows, value):
        fa[rows, :] = fa[rows, :] + value

    along_x(zb, zb, xe_ref, square)
    along_y(ye_ref, square, first)
    along_x(fa, fb, xe_ref, square)
    along_y(ye_ref, square, second)
    along_x(fc, fb, xt_ref, NUGGET)
    along_y(yt_ref, NUGGET, third)

    @pl.loop(0, BLOCKS)
    def _(b):
        side = jnp.where(b % 2 == core, 0, S // 2)
        for j in range(8):
            row = b * BLK + rows_ref[side + place_ref[b // 2] * 8 + j]
            mis[pl.ds(b * 8 + j, 1), :] = fa[pl.ds(row, 1), :]

    high = mis[...].astype(BF16)
    cat[0:S, :] = high
    cat[S : 2 * S, :] = high
    cat[2 * S : 3 * S, :] = (mis[...] - high.astype(F32)).astype(BF16)
    for gc in range(8):
        w = ymine_ref[place_ref[gc], :, S : 3 * S]
        wcat[gc * BLK : (gc + 1) * BLK, 0 : 2 * S] = w
        wcat[gc * BLK : (gc + 1) * BLK, 2 * S : 3 * S] = w[:, 0:S]
    uf[0 : 8 * BLK, :] = jnp.dot(wcat[...], cat[...], preferred_element_type=F32)

    @pl.loop(0, 8)
    def _(gc):
        row = pl.multiple_of((2 * gc + core) * BLK, BLK)
        mine = pl.multiple_of(gc * BLK, BLK)
        for pair in range(BLOCKS // 2):
            cols = slice(pair * S, (pair + 1) * S)
            a = fa[pl.ds(row, HALF), cols] - uf[pl.ds(mine, HALF), cols]
            b = fa[pl.ds(row + HALF, HALF), cols] - uf[pl.ds(mine + HALF, HALF), cols]
            out_ref[2 * pair, gc] = jnp.where(low, a, swap_halves(b)).astype(BF16)
            out_ref[2 * pair + 1, gc] = jnp.where(low, swap_halves(a), b).astype(BF16)


def sample_all(place, coeff, rows, own, other, xt, xe, yt, ye, ymine):
    smem = pl.BlockSpec(memory_space=SMEM)
    vmem = pl.BlockSpec(memory_space=VMEM)
    return pl.pallas_call(
        sample_kernel,
        out_shape=jax.ShapeDtypeStruct((16, 8, HALF, S), BF16),
        in_specs=[smem, smem, smem] + [vmem] * 7,
        out_specs=vmem,
        scratch_shapes=[
            VMEM((N, N), BF16),
            VMEM((N, N), BF16),
            VMEM((N, N), F32),
            VMEM((N, N), BF16),
            VMEM((N, N), F32),
            VMEM((N, N), F32),
            VMEM((S, N), F32),
            VMEM((3 * S, N), BF16),
            VMEM((8 * BLK, 3 * S), BF16),
        ],
        compiler_params=pltpu.CompilerParams(vmem_limit_bytes=28 * 1024 * 1024),
        cost_estimate=pl.CostEstimate(
            flops=6 * 2 * N * N * 512, bytes_accessed=5 * 1024 * 1024, transcendentals=0
        ),
        name="sample_all",
    )(place, coeff, rows, own, other, xt, xe, yt, ye, ymine)


def gather_ring(value, axis):
    size = lax.axis_size(axis)
    parts = [value] + [
        lax.ppermute(value, axis, [(i, (i + step) % size) for i in range(size)])
        for step in range(1, size)
    ]
    return jnp.stack(parts)


def body(noise, cheb_coeff, diag_x, couple_x, diag_y, couple_y, track_rows, track_obs, weights):
    core = lax.axis_index("core")
    y = lax.axis_index("y")
    zl = lax.axis_index("zl")
    chips = ("zh", "x", "y", "zl")

    xpay, ypay = payloads(
        (y * 4 + zl * 2 + core).reshape(1).astype(jnp.int32),
        track_rows,
        diag_x,
        couple_x,
        diag_y,
        couple_y,
        weights,
        track_obs,
    )
    turned = [((zh + v) % 4 * 4 + v, zh * 4 + v) for zh in range(4) for v in range(4)]
    xfar = lax.ppermute(xpay, ("zh", "y"), turned)
    yfar = gather_ring(ypay, "zl")
    sent = split_samples(noise)
    sent, xfar, yfar = lax.optimization_barrier((sent, xfar, yfar))
    own = lax.all_to_all(sent, chips, 0, 0, tiled=True)

    yfar = yfar.at[:, 16 : 16 + HALF, 3 * S : 4 * S].set(xfar.reshape(2, HALF, S))
    ymine = gather_ring(yfar, "y").reshape(8, BLK, 4 * S)
    xfar = ymine[:, 16 : 16 + HALF, 3 * S : 4 * S].reshape(4, BLK, S)
    xmats = gather_ring(xfar, "x").reshape(16, BLK, S)
    ytheirs = lax.ppermute(ymine, "core", [(0, 1), (1, 0)])
    own, xmats, ymine, ytheirs = lax.optimization_barrier((own, xmats, ymine, ytheirs))
    other = lax.ppermute(own, "core", [(0, 1), (1, 0)])

    index = jnp.arange(16, dtype=jnp.int32)
    near = (lax.axis_index("x") - index % 4) % 4
    far = (y + lax.axis_index("zh") - index // 4) % 4
    spot = (y - index // 2) % 4 * 2 + (zl - index) % 2
    spot = jnp.where(index == 8, core, spot)
    place = jnp.concatenate([spot, near * 4 + far]).astype(jnp.int32)
    xt, xe, yt, ye = bands(place, xmats, ymine, ytheirs)
    extras = jnp.stack([ymine, ytheirs])[:, :, 0:16, 3 * S : 4 * S]
    rows = extras[:, :, 8:16, BLK].astype(jnp.int32).reshape(S)

    shape = (16, 8, HALF, S)
    result = sample_all(
        place,
        cheb_coeff,
        rows,
        own.reshape(shape),
        other.reshape(shape),
        xt,
        xe,
        yt,
        ye,
        ymine,
    )
    back = lax.all_to_all(result.reshape(S, HALF, S), chips, 0, 0, tiled=True)

    parts = extras.astype(F32)
    obs = parts[:, :, 0:8, 0:BLK] + parts[:, :, 0:8, BLK:S] + parts[:, :, 8:16, 0:BLK]
    block = jnp.arange(16, dtype=jnp.int32)
    spot = (y - block // 4) % 4 * 2 + (zl - block // 2) % 2
    spot = jnp.where(block % 2 == core, spot, spot + 8)
    order = (spot[:, None] == block[None, :]).astype(F32)
    obs = jnp.dot(order, obs.reshape(16, 8 * BLK), precision=lax.Precision.HIGHEST)
    extra = jnp.dot(
        weights,
        obs.reshape(S, BLK),
        precision=lax.Precision.HIGHEST,
        preferred_element_type=F32,
    )
    return join_samples(back, extra)


def solution(mesh):
    fine = Mesh(mesh.devices.reshape(4, 4, 4, 2, 2), ("zh", "x", "y", "zl", "core"))
    rows = ("y", "zl", "core")
    cols = ("zh", "x")
    return jax.shard_map(
        body,
        mesh=fine,
        in_specs=(
            P(rows, cols, None),
            P(),
            P(cols, None),
            P(cols, None),
            P(rows, None),
            P(rows, None),
            P(rows),
            P(rows, cols),
            P(rows, None),
        ),
        out_specs=P(rows, cols, None),
        check_vma=False,
    )
```

```python
import functools

import jax
import jax.numpy as jnp
from jax import lax
from jax.experimental import pallas as pl
from jax.experimental.pallas import tpu as pltpu
from jax.sharding import Mesh, PartitionSpec as P

NUGGET = 0.3
BLK = 64
HALF = 32
N = 1024
S = 128
TILE = 256
TILES = N // TILE
BLOCKS = N // BLK
F32 = jnp.float32
BF16 = jnp.bfloat16
VMEM = pltpu.VMEM
SMEM = pltpu.SMEM


def low_lanes(shape):
    return lax.broadcasted_iota(jnp.int32, shape, len(shape) - 1) < BLK


def swap_halves(value):
    return pltpu.roll(value, BLK, axis=1)


def split_samples_kernel(noise_ref, out_ref, tmp_ref):
    rows = out_ref.shape[1]
    for k in range(rows):
        pair = jnp.concatenate([noise_ref[0, k], noise_ref[1, k]], axis=0).astype(F32)
        tmp_ref[pl.ds(k, S, stride=rows), :] = pair.T
    out_ref[...] = tmp_ref[...].reshape(S, rows, S).astype(BF16)


def split_samples(noise):
    rows = 8
    return pl.pallas_call(
        split_samples_kernel,
        grid=(HALF // rows,),
        out_shape=jax.ShapeDtypeStruct((S, HALF, S), BF16),
        in_specs=[pl.BlockSpec((2, rows, BLK, S), lambda i: (0, i, 0, 0))],
        out_specs=pl.BlockSpec((S, rows, S), lambda i: (0, i, 0)),
        scratch_shapes=[VMEM((S * rows, S), F32)],
        compiler_params=pltpu.CompilerParams(vmem_limit_bytes=60 * 1024 * 1024),
        cost_estimate=pl.CostEstimate(flops=0, bytes_accessed=2 * 1024 * 1024, transcendentals=0),
        name="split_samples",
    )(noise.reshape(2, HALF, BLK, S))


def join_samples_kernel(msg_ref, extra_ref, out_ref, tmp_ref):
    rows = msg_ref.shape[1]
    tmp_ref[...] = msg_ref[...].astype(F32).reshape(S * rows, S)
    extra = extra_ref[0]
    for k in range(rows):
        pair = tmp_ref[pl.ds(k, S, stride=rows), :].T
        for yh in range(2):
            column = extra[:, yh * rows + k : yh * rows + k + 1]
            out_ref[yh, k] = pair[yh * BLK : (yh + 1) * BLK] + column


def join_samples(msg, extra):
    rows = 16
    steps = HALF // rows
    cols = extra.reshape(2, steps, rows, BLK).transpose(1, 3, 0, 2).reshape(steps, BLK, 2 * rows)
    out = pl.pallas_call(
        join_samples_kernel,
        grid=(steps,),
        out_shape=jax.ShapeDtypeStruct((2, HALF, BLK, S), F32),
        in_specs=[
            pl.BlockSpec((S, rows, S), lambda i: (0, i, 0)),
            pl.BlockSpec((1, BLK, 2 * rows), lambda i: (i, 0, 0)),
        ],
        out_specs=pl.BlockSpec((2, rows, BLK, S), lambda i: (0, i, 0, 0)),
        scratch_shapes=[VMEM((S * rows, S), F32)],
        compiler_params=pltpu.CompilerParams(vmem_limit_bytes=16 * 1024 * 1024),
        cost_estimate=pl.CostEstimate(flops=0, bytes_accessed=3 * 1024 * 1024, transcendentals=0),
        name="join_samples",
    )(msg, cols)
    return out.reshape(BLK, BLK, S)


def payload_kernel(
    block_ref, track_ref, dx_ref, kx_ref, dy_ref, ky_ref, weights_ref, obs_ref, x_ref, y_ref
):
    x_ref[...] = jnp.concatenate([dx_ref[...].T, kx_ref[...].astype(F32)], axis=1).astype(BF16)
    y_ref[:, 0:S] = jnp.concatenate([dy_ref[...], ky_ref[...].astype(F32)], axis=1).astype(BF16)
    weights = weights_ref[...]
    high = weights.astype(BF16)
    y_ref[:, S : 2 * S] = high
    y_ref[:, 2 * S : 3 * S] = (weights - high.astype(F32)).astype(BF16)
    obs = obs_ref[...]
    one = obs.astype(BF16).astype(F32)
    two = (obs - one).astype(BF16).astype(F32)
    three = obs - one - two
    row = lax.broadcasted_iota(jnp.int32, (8, BLK), 0)
    local = jnp.zeros((8, BLK), F32)
    for j in range(8):
        local = jnp.where(row == j, (track_ref[j] - block_ref[0] * BLK).astype(F32), local)
    extra = jnp.concatenate(
        [
            jnp.concatenate([one, two], axis=1),
            jnp.concatenate([three, local], axis=1),
            jnp.zeros((BLK - 16, S), F32),
        ],
        axis=0,
    )
    y_ref[:, 3 * S : 4 * S] = extra.astype(BF16)


def payloads(block, tracks, dx, kx, dy, ky, weights, obs):
    smem = pl.BlockSpec(memory_space=SMEM)
    vmem = pl.BlockSpec(memory_space=VMEM)
    return pl.pallas_call(
        payload_kernel,
        out_shape=(
            jax.ShapeDtypeStruct((BLK, S), BF16),
            jax.ShapeDtypeStruct((BLK, 4 * S), BF16),
        ),
        in_specs=[smem, smem] + [vmem] * 6,
        out_specs=(vmem, vmem),
        name="payloads",
    )(block, tracks, dx, kx, dy, ky, weights, obs)


def reach(t):
    return max(0, t * TILE - S), min(N, (t + 1) * TILE + S)


def base(t):
    return t * TILE - S


def band_kernel(
    place_ref, x_ref, mine_ref, theirs_ref, xt_ref, xe_ref, yt_ref, ye_ref, dense
):
    dense[...] = jnp.zeros_like(dense)
    zero = jnp.zeros((BLK, BLK), F32)

    def put(row, pair, left, right):
        dense[row * BLK : (row + 1) * BLK, pair * S : (pair + 1) * S] = jnp.concatenate(
            [left, right], axis=1
        ).astype(BF16)

    def x_block(b):
        return x_ref[place_ref[16 + b], :, 0:S].astype(F32)

    def y_block(b):
        spot = place_ref[b // 2]
        own = mine_ref[spot, :, 0:S].astype(F32)
        other = theirs_ref[spot, :, 0:S].astype(F32)
        return jnp.where(place_ref[8] == b % 2, own, other)

    def split(both):
        return both[:, 0:BLK], both[:, BLK:S], both.T[BLK:S, :]

    for block, t_ref, e_ref in ((x_block, xt_ref, xe_ref), (y_block, yt_ref, ye_ref)):
        for pair in range(BLOCKS // 2):
            even, odd = 2 * pair, 2 * pair + 1
            d_even, k_even, back_even = split(block(even))
            d_odd, k_odd, back_odd = split(block(odd))
            put(even, pair, d_even, back_odd)
            put(odd, pair, k_odd, d_odd)
            if pair > 0:
                put(even - 1, pair, back_even, zero)
                put(even, pair - 1, zero, k_even)
        for t in range(TILES):
            lo, hi = reach(t)
            near = slice(lo - base(t), hi - base(t))
            one = dense[lo:hi, t * TILE : (t + 1) * TILE]
            two = jnp.dot(dense[lo:hi, lo:hi], one, preferred_element_type=F32)
            t_ref[t, near, :] = one
            e_ref[t, near, :] = ((2.0 * NUGGET) * one.astype(F32) + two).astype(BF16)


def bands(place, xmats, mine, theirs):
    vmem = pl.BlockSpec(memory_space=VMEM)
    return pl.pallas_call(
        band_kernel,
        out_shape=(jax.ShapeDtypeStruct((TILES, 2 * TILE, TILE), BF16),) * 4,
        in_specs=[pl.BlockSpec(memory_space=SMEM), vmem, vmem, vmem],
        out_specs=(vmem,) * 4,
        scratch_shapes=[VMEM((N, N), BF16)],
        compiler_params=pltpu.CompilerParams(vmem_limit_bytes=16 * 1024 * 1024),
        cost_estimate=pl.CostEstimate(
            flops=4 * 4 * TILE * TILE * 4 * TILE, bytes_accessed=6 * 1024 * 1024, transcendentals=0
        ),
        name="bands",
    )(place, xmats, mine, theirs)


def sample_kernel(
    place_ref,
    coeff_ref,
    rows_ref,
    own_ref,
    other_ref,
    xt_ref,
    xe_ref,
    yt_ref,
    ye_ref,
    ymine_ref,
    out_ref,
    zb,
    fb,
    uf,
    ub,
    fa,
    fc,
    mis,
    cat,
    wcat,
):
    core = place_ref[8]
    low = low_lanes((HALF, S))

    @pl.loop(0, 8)
    def _(gc):
        for ref, parity in ((own_ref, core), (other_ref, 1 - core)):
            row = pl.multiple_of((2 * gc + parity) * BLK, BLK)
            for pair in range(BLOCKS // 2):
                a = ref[2 * pair, gc].astype(F32)
                b = ref[2 * pair + 1, gc].astype(F32)
                cols = slice(pair * S, (pair + 1) * S)
                zb[pl.ds(row, HALF), cols] = jnp.where(low, a, swap_halves(b)).astype(BF16)
                zb[pl.ds(row + HALF, HALF), cols] = jnp.where(low, swap_halves(a), b).astype(BF16)

    def along_x(source, source_b, band, share):
        for t in range(TILES):
            lo, hi = reach(t)
            cols = slice(t * TILE, (t + 1) * TILE)
            matrix = band[t, lo - base(t) : hi - base(t), :]
            part = jnp.dot(source_b[:, lo:hi], matrix, preferred_element_type=F32)
            value = share * source[:, cols].astype(F32) + part
            uf[:, cols] = value
            ub[:, cols] = value.astype(BF16)

    def along_y(band, share, finish):
        for k in range(TILES):
            lo, hi = reach(k)
            matrix = band[k, lo - base(k) : hi - base(k), :]
            part = jnp.dot(matrix, ub[k * TILE : (k + 1) * TILE, :], preferred_element_type=F32)
            for j in range(lo // S, hi // S):
                rows = slice(j * S, (j + 1) * S)
                value = part[j * S - lo : (j + 1) * S - lo]
                if k == max(0, (j - 1) // 2):
                    value = share * uf[rows, :] + value
                else:
                    value = uf[rows, :] + value
                if k == min(TILES - 1, (j + 1) // 2):
                    finish(rows, value)
                else:
                    uf[rows, :] = value

    c = [coeff_ref[i] for i in range(6)]
    square = NUGGET * NUGGET

    def first(rows, value):
        value = 2.0 * value - zb[rows, :].astype(F32)
        fa[rows, :] = value
        fb[rows, :] = value.astype(BF16)

    def second(rows, value):
        once = fa[rows, :]
        start = zb[rows, :].astype(F32)
        twice = 2.0 * value - once
        fa[rows, :] = (c[0] - c[4]) * start + c[2] * once + (2.0 * c[4]) * twice
        odd = (c[1] - c[3] - c[5]) * start + (2.0 * (c[3] - c[5])) * once + (4.0 * c[5]) * twice
        fc[rows, :] = odd
        fb[rows, :] = odd.astype(BF16)

    def third(rows, value):
        fa[rows, :] = fa[rows, :] + value

    along_x(zb, zb, xe_ref, square)
    along_y(ye_ref, square, first)
    along_x(fa, fb, xe_ref, square)
    along_y(ye_ref, square, second)
    along_x(fc, fb, xt_ref, NUGGET)
    along_y(yt_ref, NUGGET, third)

    @pl.loop(0, BLOCKS)
    def _(b):
        side = jnp.where(b % 2 == core, 0, S // 2)
        for j in range(8):
            row = b * BLK + rows_ref[side + place_ref[b // 2] * 8 + j]
            mis[pl.ds(b * 8 + j, 1), :] = fa[pl.ds(row, 1), :]

    high = mis[...].astype(BF16)
    cat[0:S, :] = high
    cat[S : 2 * S, :] = high
    cat[2 * S : 3 * S, :] = (mis[...] - high.astype(F32)).astype(BF16)
    for gc in range(8):
        w = ymine_ref[place_ref[gc], :, S : 3 * S]
        wcat[gc * BLK : (gc + 1) * BLK, 0 : 2 * S] = w
        wcat[gc * BLK : (gc + 1) * BLK, 2 * S : 3 * S] = w[:, 0:S]
    uf[0 : 8 * BLK, :] = jnp.dot(wcat[...], cat[...], preferred_element_type=F32)

    @pl.loop(0, 8)
    def _(gc):
        row = pl.multiple_of((2 * gc + core) * BLK, BLK)
        mine = pl.multiple_of(gc * BLK, BLK)
        for pair in range(BLOCKS // 2):
            cols = slice(pair * S, (pair + 1) * S)
            a = fa[pl.ds(row, HALF), cols] - uf[pl.ds(mine, HALF), cols]
            b = fa[pl.ds(row + HALF, HALF), cols] - uf[pl.ds(mine + HALF, HALF), cols]
            out_ref[2 * pair, gc] = jnp.where(low, a, swap_halves(b)).astype(BF16)
            out_ref[2 * pair + 1, gc] = jnp.where(low, swap_halves(a), b).astype(BF16)


def sample_all(place, coeff, rows, own, other, xt, xe, yt, ye, ymine):
    smem = pl.BlockSpec(memory_space=SMEM)
    vmem = pl.BlockSpec(memory_space=VMEM)
    return pl.pallas_call(
        sample_kernel,
        out_shape=jax.ShapeDtypeStruct((16, 8, HALF, S), BF16),
        in_specs=[smem, smem, smem] + [vmem] * 7,
        out_specs=vmem,
        scratch_shapes=[
            VMEM((N, N), BF16),
            VMEM((N, N), BF16),
            VMEM((N, N), F32),
            VMEM((N, N), BF16),
            VMEM((N, N), F32),
            VMEM((N, N), F32),
            VMEM((S, N), F32),
            VMEM((3 * S, N), BF16),
            VMEM((8 * BLK, 3 * S), BF16),
        ],
        compiler_params=pltpu.CompilerParams(vmem_limit_bytes=28 * 1024 * 1024),
        cost_estimate=pl.CostEstimate(
            flops=6 * 2 * N * N * 512, bytes_accessed=5 * 1024 * 1024, transcendentals=0
        ),
        name="sample_all",
    )(place, coeff, rows, own, other, xt, xe, yt, ye, ymine)


def gather_ring(value, axis):
    size = lax.axis_size(axis)
    parts = [value] + [
        lax.ppermute(value, axis, [(i, (i + step) % size) for i in range(size)])
        for step in range(1, size)
    ]
    return jnp.stack(parts)


def body(noise, cheb_coeff, diag_x, couple_x, diag_y, couple_y, track_rows, track_obs, weights):
    core = lax.axis_index("core")
    y = lax.axis_index("y")
    zl = lax.axis_index("zl")
    chips = ("zh", "x", "y", "zl")

    xpay, ypay = payloads(
        (y * 4 + zl * 2 + core).reshape(1).astype(jnp.int32),
        track_rows,
        diag_x,
        couple_x,
        diag_y,
        couple_y,
        weights,
        track_obs,
    )
    turned = [((zh + v) % 4 * 4 + v, zh * 4 + v) for zh in range(4) for v in range(4)]
    xfar = lax.ppermute(xpay, ("zh", "y"), turned)
    yfar = gather_ring(ypay, "zl")
    sent = split_samples(noise)
    sent, xfar, yfar = lax.optimization_barrier((sent, xfar, yfar))
    own = lax.all_to_all(sent, chips, 0, 0, tiled=True)

    yfar = yfar.at[:, 16 : 16 + HALF, 3 * S : 4 * S].set(xfar.reshape(2, HALF, S))
    ymine = gather_ring(yfar, "y").reshape(8, BLK, 4 * S)
    xfar = ymine[:, 16 : 16 + HALF, 3 * S : 4 * S].reshape(4, BLK, S)
    xmats = gather_ring(xfar, "x").reshape(16, BLK, S)
    ytheirs = lax.ppermute(ymine, "core", [(0, 1), (1, 0)])
    own, xmats, ymine, ytheirs = lax.optimization_barrier((own, xmats, ymine, ytheirs))
    other = lax.ppermute(own, "core", [(0, 1), (1, 0)])

    index = jnp.arange(16, dtype=jnp.int32)
    near = (lax.axis_index("x") - index % 4) % 4
    far = (y + lax.axis_index("zh") - index // 4) % 4
    spot = (y - index // 2) % 4 * 2 + (zl - index) % 2
    spot = jnp.where(index == 8, core, spot)
    place = jnp.concatenate([spot, near * 4 + far]).astype(jnp.int32)
    xt, xe, yt, ye = bands(place, xmats, ymine, ytheirs)
    extras = jnp.stack([ymine, ytheirs])[:, :, 0:16, 3 * S : 4 * S]
    rows = extras[:, :, 8:16, BLK].astype(jnp.int32).reshape(S)

    shape = (16, 8, HALF, S)
    result = sample_all(
        place,
        cheb_coeff,
        rows,
        own.reshape(shape),
        other.reshape(shape),
        xt,
        xe,
        yt,
        ye,
        ymine,
    )
    back = lax.all_to_all(result.reshape(S, HALF, S), chips, 0, 0, tiled=True)

    parts = extras.astype(F32)
    obs = parts[:, :, 0:8, 0:BLK] + parts[:, :, 0:8, BLK:S] + parts[:, :, 8:16, 0:BLK]
    block = jnp.arange(16, dtype=jnp.int32)
    spot = (y - block // 4) % 4 * 2 + (zl - block // 2) % 2
    spot = jnp.where(block % 2 == core, spot, spot + 8)
    order = (spot[:, None] == block[None, :]).astype(F32)
    obs = jnp.dot(order, obs.reshape(16, 8 * BLK), precision=lax.Precision.HIGHEST)
    extra = jnp.dot(
        weights,
        obs.reshape(S, BLK),
        precision=lax.Precision.HIGHEST,
        preferred_element_type=F32,
    )
    return join_samples(back, extra)


def solution(mesh):
    fine = Mesh(mesh.devices.reshape(4, 4, 4, 2, 2), ("zh", "x", "y", "zl", "core"))
    rows = ("y", "zl", "core")
    cols = ("zh", "x")
    return jax.shard_map(
        body,
        mesh=fine,
        in_specs=(
            P(rows, cols, None),
            P(),
            P(cols, None),
            P(cols, None),
            P(rows, None),
            P(rows, None),
            P(rows),
            P(rows, cols),
            P(rows, None),
        ),
        out_specs=P(rows, cols, None),
        check_vma=False,
    )
```
